128 devices in a mesh: cells: 128 (over z, y, x, core).
Axes of the slice: x: 4, y: 4, z: 4, core: 2. Of those that a mesh axis runs over, the one named last changes fastest.
Arguments:
- multipoles: bfloat16 [216, 131072], P(None, 'cells'), may hold values from -6 to 6
- compress: bfloat16 [216, 128], replicated, may hold values from -0.4375 to 0.4375
- operators: bfloat16 [316, 128, 128], replicated, may hold values from -0.0390625 to 0.0390625
- expand: bfloat16 [128, 216], replicated, may hold values from -0.5 to 0.5
Outputs:
- local_field: float32 [216, 131072], P(None, 'cells')
The draws below stay inside these ranges and needn't reach their ends.
All inputs are finite; a program needn't handle non-finite values.
Results may differ from the reference program's by a relative error of at most 0.0041.
Values may be sent and summed in bfloat16 or wider, within the bound.
No kernel may reach another device: no remote copies, remote signals or barrier semaphores. Data moves between devices by JAX's collectives and lax.ppermute only.
A program may use at most 256 MiB of HBM per device.

```python
import jax
import jax.numpy as jnp
import numpy as np
from jax import lax

CHEB = 216
RANK = 128
OFFSETS = 316
LIST = 189
CELLS = 131072


def block_levels(own_key, extent, cuts, smallest, largest):
    def one(axis_at, blocks):
        heights = jax.random.uniform(jax.random.fold_in(jax.random.fold_in(own_key, 6), axis_at), (blocks,), jnp.float32, smallest / len(cuts), largest / len(cuts))
        return jnp.repeat(jnp.exp(heights), extent[axis_at] // blocks).reshape((-1,) + (1,) * (len(extent) - axis_at - 1))

    factor_of = one(*cuts[0])
    for cut in cuts[1:]:
        factor_of = factor_of * one(*cut)
    return factor_of


def bell_draw(key, shape, scale, limit, cuts=(), kind=jnp.bfloat16):
    values = scale * jax.random.normal(key, shape, jnp.float32)
    if cuts:
        values = values * block_levels(key, shape, cuts, -0.22, 0.18)
    return jnp.clip(values, -limit, limit).astype(kind)


def setup_inputs(seed: int = 0) -> dict:
    splits = jax.random.split(jax.random.key(seed), 5)
    return {
        "multipoles": bell_draw(splits[0], (CHEB, CELLS), 1.0, 6.0, ((1, 128),)),
        "compress": bell_draw(splits[1], (CHEB, RANK), CHEB ** -0.5, 0.4375),
        "operators": bell_draw(splits[2], (OFFSETS, RANK, RANK), (LIST * RANK) ** -0.5, 0.0390625),
        "expand": bell_draw(splits[3], (RANK, CHEB), RANK ** -0.5, 0.5),
    }


def offset_list():
    result = []
    for shift_x in range(-3, 4):
        for shift_y in range(-3, 4):
            for shift_z in range(-3, 4):
                if max(abs(shift_x), abs(shift_y), abs(shift_z)) >= 2:
                    result.append((shift_x, shift_y, shift_z))
    return result


def allowed_shifts(parity):
    return [shift for shift in range(-3, 4) if abs((parity + shift) // 2 - parity // 2) <= 1]


def grid_order(bit_count):
    axes_by_dim = [[axis_number for axis_number in range(bit_count) if (bit_count - 1 - axis_number) % 3 == dimension] for dimension in range(3)]
    order = axes_by_dim[0] + axes_by_dim[1] + axes_by_dim[2]
    return order, [len(entries) for entries in axes_by_dim]


def to_grid(flat_rows, bit_count):
    order, bit_totals = grid_order(bit_count)
    rank_width = flat_rows.shape[-1]
    shaped = flat_rows.reshape([2] * bit_count + [rank_width])
    shaped = jnp.transpose(shaped, order + [bit_count])
    return shaped.reshape([2 ** bit_total for bit_total in bit_totals] + [rank_width])


def to_flat(grid_rows, bit_count):
    order, bit_totals = grid_order(bit_count)
    rank_width = grid_rows.shape[-1]
    shaped = grid_rows.reshape([2] * bit_count + [rank_width])
    inverse = [int(entry) for entry in np.argsort(np.array(order))] + [bit_count]
    return jnp.transpose(shaped, inverse).reshape(2 ** bit_count, rank_width)


def reference(multipoles, compress, operators, expand):
    bit_count = CELLS.bit_length() - 1
    compressed = lax.dot_general(multipoles, compress, (((0,), (0,)), ((), ())), preferred_element_type=jnp.float32).astype(jnp.bfloat16)
    grid_field = to_grid(compressed.astype(jnp.float32), bit_count)
    side_x, side_y, side_z, rank_width = grid_field.shape
    half_x, half_y, half_z = side_x // 2, side_y // 2, side_z // 2
    padded = jnp.pad(grid_field, ((2, 2), (2, 2), (2, 2), (0, 0)))
    parity_split = padded.reshape(half_x + 2, 2, half_y + 2, 2, half_z + 2, 2, rank_width)
    weights = operators.astype(jnp.float32)
    lookup = {triple: offset_id for offset_id, triple in enumerate(offset_list())}
    pieces = []
    for parity_x in range(2):
        for parity_y in range(2):
            for parity_z in range(2):
                starts = []
                offset_ids = []
                for shift_x in allowed_shifts(parity_x):
                    for shift_y in allowed_shifts(parity_y):
                        for shift_z in allowed_shifts(parity_z):
                            triple = (shift_x, shift_y, shift_z)
                            if triple in lookup:
                                start_x = 2 + parity_x + shift_x
                                start_y = 2 + parity_y + shift_y
                                start_z = 2 + parity_z + shift_z
                                starts.append([start_x // 2, start_x % 2, start_y // 2, start_y % 2, start_z // 2, start_z % 2])
                                offset_ids.append(lookup[triple])
                start_table = jnp.asarray(np.array(starts, dtype=np.int32))
                id_table = jnp.asarray(np.array(offset_ids, dtype=np.int32))

                def accumulate(summed, entry_pair):
                    start_row, offset_id = entry_pair
                    source = lax.dynamic_slice(parity_split, (start_row[0], start_row[1], start_row[2], start_row[3], start_row[4], start_row[5], jnp.int32(0)), (half_x, 1, half_y, 1, half_z, 1, rank_width))
                    source = source.reshape(half_x * half_y * half_z, rank_width)
                    matrix = lax.dynamic_index_in_dim(weights, offset_id, 0, keepdims=False)
                    return summed + jnp.dot(source, matrix, precision=lax.Precision.HIGHEST, preferred_element_type=jnp.float32), None

                initial = jnp.zeros((half_x * half_y * half_z, rank_width), jnp.float32)
                summed, unused = lax.scan(accumulate, initial, (start_table, id_table))
                pieces.append(summed.reshape(half_x, half_y, half_z, rank_width))
    stacked = jnp.stack(pieces).reshape(2, 2, 2, half_x, half_y, half_z, rank_width)
    whole_grid = jnp.transpose(stacked, (3, 0, 4, 1, 5, 2, 6)).reshape(side_x, side_y, side_z, rank_width)
    reduced = to_flat(whole_grid, bit_count).astype(jnp.bfloat16)
    return lax.dot_general(expand, reduced, (((0,), (1,)), ((), ())), preferred_element_type=jnp.float32)
```

```python
import functools

import jax
import jax.numpy as jnp
import numpy as np
from jax import lax
from jax.experimental import pallas as pl
from jax.experimental.pallas import tpu as pltpu
from jax.sharding import PartitionSpec as P

RANK = 128
BF = jnp.bfloat16
F32 = jnp.float32
OWN, X_ROWS, Y_ROWS, Z_ROWS = 128, 16, 48, 64
X_BASE = OWN
Y_BASE = X_BASE + 2 * X_ROWS
Z_BASE = Y_BASE + 2 * Y_ROWS
TABLE = Z_BASE + 2 * Z_ROWS
PIECES = 4
Y_TABLE, Z_TABLE, INNER_TABLE, OUTER_TABLE = 0, 96, 224, 736

OFFSETS = [
    (dx, dy, dz)
    for dx in range(-3, 4)
    for dy in range(-3, 4)
    for dz in range(-3, 4)
    if max(abs(dx), abs(dy), abs(dz)) >= 2
]
LOOKUP = {triple: number for number, triple in enumerate(OFFSETS)}
TARGETS = [(0, 0), (0, 1), (1, 0), (1, 1)]


def table_row(bits, sub):
    (x0, y0, z0), (sx, sy, sz) = bits, sub
    xi, yi = sx + x0, sy + y0
    if sz in (-1, 2):
        return Z_BASE + (sz == 2) * Z_ROWS + (x0 + 2 * y0) * 15 + xi + 5 * yi
    if sy in (-1, 2):
        return Y_BASE + (sy == 2) * Y_ROWS + (x0 + 2 * z0) * 10 + xi + 5 * sz
    if sx in (-1, 4):
        return X_BASE + (sx == 4) * X_ROWS + (y0 + 2 * z0) * 4 + sy + 2 * sz
    return (x0 + 2 * y0 + 4 * z0) * 16 + (sx & 1) + 2 * sy + 4 * sz + 8 * (sx >> 1)


def one_hot(sources, width):
    table = np.zeros((len(sources), width), np.float32)
    for row, source in enumerate(sources):
        if source is not None:
            table[row, source] = 1.0
    return table


def send_table(dimension, rows, width):
    top = (3, 1, 1)[dimension]
    result = [None] * (2 * rows)
    base = (X_BASE, Y_BASE, Z_BASE)[dimension]
    for upward in (1, 0):
        for number in range(8):
            bits = (number & 1, number >> 1 & 1, number >> 2 & 1)
            if bits[dimension] != upward:
                continue
            ranges = [range(-b, n + 1 - b) if d < dimension else range(n) for d, (b, n) in enumerate(zip(bits, (4, 2, 2)))]
            ranges[dimension] = [top if upward else 0]
            for sx in ranges[0]:
                for sy in ranges[1]:
                    for sz in ranges[2]:
                        here = [sx, sy, sz]
                        there = list(here)
                        there[dimension] = -1 if upward else top + 1
                        landing = table_row(bits, there) - base
                        assert landing // rows == 1 - upward
                        result[landing] = table_row(bits, here)
    return one_hot(result, width)


def window_table(planes):
    sources = []
    for px in range(4):
        for py in range(4):
            for pz in planes:
                for sb in range(16):
                    sub = ((sb & 1) + 2 * (sb >> 3), sb >> 1 & 1, sb >> 2 & 1)
                    place = [2 * s + p - 1 for s, p in zip(sub, (px, py, pz))]
                    sources.append(table_row([v & 1 for v in place], [v >> 1 for v in place]))
    return one_hot(sources, TABLE)


def matmul(a, b):
    return jnp.dot(a, b, preferred_element_type=F32)


def pick(even, sent, rows, to_even, to_odd):
    to_even[...] = sent[pl.ds(pl.multiple_of((1 - even) * rows, rows), rows), :]
    to_odd[...] = sent[pl.ds(pl.multiple_of(even * rows, rows), rows), :]


def place(even, from_even, from_odd, rows, landed):
    landed[pl.ds(pl.multiple_of(even * rows, rows), rows), :] = from_even[...]
    landed[pl.ds(pl.multiple_of((1 - even) * rows, rows), rows), :] = from_odd[...]


def x_picks():
    row = lax.broadcasted_iota(jnp.int32, (2 * X_ROWS, OWN), 0)
    column = lax.broadcasted_iota(jnp.int32, (2 * X_ROWS, OWN), 1)
    upward = 1 - (row >> 4)
    source = upward * 25 + (row >> 2 & 1) * 32 + (row >> 3 & 1) * 64 + (row & 1) * 2 + (row >> 1 & 1) * 4
    return jnp.where(column == source, 1.0, 0.0).astype(BF)


def compress_kernel(even, multipoles_hbm, compress_hbm, own, to_even, to_odd, multipoles, compress, rows, sent, sem):
    copies = [
        pltpu.make_async_copy(multipoles_hbm, multipoles, sem.at[0]),
        pltpu.make_async_copy(compress_hbm, compress, sem.at[1]),
    ]
    for copy in copies:
        copy.start()
    for copy in copies:
        copy.wait()
    rows[...] = lax.dot_general(
        multipoles[...], compress[...], (((0,), (0,)), ((), ())), preferred_element_type=F32
    )
    for number in range(8):
        for child in range(8):
            x0, y0, z0 = child & 1, child >> 1 & 1, child >> 2 & 1
            lane = ((x0 * 2 + y0) * 2 + z0) * RANK
            own[number * 16 : number * 16 + 16, lane : lane + RANK] = rows[
                pl.ds(number * 8 + child, 16, stride=64), :
            ].astype(BF)
    sent[...] = matmul(x_picks(), own[...]).astype(BF)
    pick(even[0], sent, X_ROWS, to_even, to_odd)


def stage_kernel(own, ops_hbm, table_hbm, ops, table, token, sem):
    pieces = [(table_hbm, table)]
    size = ops.shape[0] // PIECES
    for piece in range(PIECES):
        here = pl.ds(piece * size, size)
        pieces.append((ops_hbm.at[here], ops.at[here]))
    copies = [pltpu.make_async_copy(*piece, sem.at[i]) for i, piece in enumerate(pieces)]
    for copy in copies:
        copy.start()
    token[...] = jnp.zeros_like(token)
    for copy in copies:
        copy.wait()


def forward(table, own, landed, sent):
    rows, width = sent.shape[0], OWN + landed.shape[0]
    picks = table[:rows, :width]
    sent[...] = (matmul(picks[:, :OWN], own[...]) + matmul(picks[:, OWN:], landed[...])).astype(BF)


def forward_y_kernel(even, own, xe, xo, table, token, to_even, to_odd, landed, sent):
    place(even[0], xe, xo, X_ROWS, landed)
    forward(table.at[Y_TABLE:Z_TABLE], own, landed, sent)
    pick(even[1], sent, Y_ROWS, to_even, to_odd)


def forward_z_kernel(even, own, xe, xo, ye, yo, table, to_even, to_odd, landed, sent):
    place(even[0], xe, xo, X_ROWS, landed.at[0 : 2 * X_ROWS])
    place(even[1], ye, yo, Y_ROWS, landed.at[2 * X_ROWS :])
    forward(table.at[Z_TABLE:INNER_TABLE], own, landed, sent)
    pick(even[2], sent, Z_ROWS, to_even, to_odd)


def parity_shift(parity, distance):
    total = parity + distance
    return (total & 1, total >> 1) if abs(total >> 1) <= 1 else None


def operator_tiles(ops, dx, dy):
    base = LOOKUP[(dx, dy, -3)] * RANK
    if max(abs(dx), abs(dy)) >= 2:
        return [
            jnp.concatenate(
                [ops[first + RANK : first + 3 * RANK, :], ops[first : first + 2 * RANK, :]], axis=1
            )
            for first in (base, base + 2 * RANK, base + 4 * RANK)
        ]
    zero = jnp.zeros((RANK, RANK), BF)
    op = {dz: ops[base + i * RANK : base + (i + 1) * RANK, :] for i, dz in enumerate((-3, -2, 2, 3))}
    below = jnp.concatenate(
        [jnp.concatenate([op[-2], op[-3]], axis=1), jnp.concatenate([zero, op[-2]], axis=1)], axis=0
    )
    above = jnp.concatenate(
        [jnp.concatenate([op[2], zero], axis=1), jnp.concatenate([op[3], op[2]], axis=1)], axis=0
    )
    return [below, None, above]


def accumulate(window, ops, half, plane_of, pairs, targets, distances):
    total = None
    for dx, dy in distances:
        tiles = operator_tiles(ops, dx, dy)
        for pair in pairs:
            if tiles[pair] is None:
                continue
            parts = []
            for target in targets:
                (qx, cx), (qy, cy) = parity_shift(target[0], dx), parity_shift(target[1], dy)
                lane = (qx * 2 + qy) * 2 * RANK
                parts.append(
                    window[
                        1 + cx : 3 + cx, 1 + cy : 3 + cy, plane_of[half + pair], :, lane : lane + 2 * RANK
                    ].reshape(64, 2 * RANK)
                )
            left = jnp.concatenate(parts, axis=0) if len(parts) > 1 else parts[0]
            term = matmul(left, tiles[pair])
            total = term if total is None else total + term
    return total


def interact(window, ops, before, after, half, plane_of, pairs):
    def add(targets, distances, start):
        total = accumulate(window, ops, half, plane_of, pairs, targets, distances)
        for i, target in enumerate(targets):
            number = TARGETS.index(target)
            part = total[i * 64 : i * 64 + 64]
            after[half, number] = part if start is None else start[half, number] + part

    inner = range(-2, 3)
    add(TARGETS, [(dx, dy) for dx in inner for dy in inner], before)
    for p in (0, 1):
        far = 3 - 6 * p
        add([(p, 0), (p, 1)], [(far, dy) for dy in inner], after)
        add([(0, p), (1, p)], [(dx, far) for dx in inner], after)
    for x0, y0 in TARGETS:
        add([(x0, y0)], [(3 - 6 * x0, 3 - 6 * y0)], after)


def fill(window, table, first, own, landed, width):
    for px in range(4):
        block = table[first + px * 128 : first + px * 128 + 128, :width]
        filled = matmul(block[:, :OWN], own[...]) + matmul(block[:, OWN:], landed[...])
        window[px] = filled.astype(BF).reshape(4, 2, 16, 8 * RANK)


def inner_kernel(even, own, xe, xo, ye, yo, table, expand, ops, acc, outer, expand_out, landed, window):
    expand_out[...] = expand[...]
    place(even[0], xe, xo, X_ROWS, landed.at[0 : 2 * X_ROWS])
    place(even[1], ye, yo, Y_ROWS, landed.at[2 * X_ROWS :])
    fill(window, table, INNER_TABLE, own, landed, Z_BASE)
    fill(outer, table, OUTER_TABLE, own, landed, Z_BASE)
    planes = {1: 0, 2: 1}
    interact(window, ops, None, acc, 0, planes, (1, 2))
    interact(window, ops, None, acc, 1, planes, (0, 1))


def outer_kernel(even, ze, zo, table, expand, ops, inner, partial, out, landed, window, acc, rows):
    place(even[2], ze, zo, Z_ROWS, landed)
    for px in range(4):
        block = table[OUTER_TABLE + px * 128 : OUTER_TABLE + px * 128 + 128, Z_BASE:]
        filled = matmul(block, landed[...]) + partial[px].reshape(128, 8 * RANK).astype(F32)
        window[px] = filled.astype(BF).reshape(4, 2, 16, 8 * RANK)
    planes = {0: 0, 3: 1}
    interact(window, ops, inner, acc, 0, planes, (0,))
    interact(window, ops, inner, acc, 1, planes, (2,))
    for number in range(8):
        first = ((number & 1) * 2 + (number >> 1 & 1)) * 16
        for child in range(8):
            x0, y0, z0 = child & 1, child >> 1 & 1, child >> 2 & 1
            rows[pl.ds(number * 8 + child, 16, stride=64), :] = acc[
                number >> 2, x0 * 2 + y0, first : first + 16, z0 * RANK : z0 * RANK + RANK
            ]
    out[...] = lax.dot_general(
        expand[...], rows[...].astype(BF), (((1,), (1,)), ((), ())), preferred_element_type=F32
    )


VMEM = pl.BlockSpec(memory_space=pltpu.VMEM)
ANY = pl.BlockSpec(memory_space=pl.ANY)
SMEM = pl.BlockSpec(memory_space=pltpu.SMEM)


def rows_of(count):
    return jax.ShapeDtypeStruct((count, 8 * RANK), BF)


def in_hbm(array):
    return pltpu.with_memory_space_constraint(array, pltpu.HBM)


def scratch(*shape, kind=BF):
    return pltpu.VMEM(shape, kind)


def call(kernel, out_shape, scratch_shapes, in_specs, limit=16 << 20, flops=1 << 24, bytes_moved=1 << 20):
    return pl.pallas_call(
        kernel,
        out_shape=out_shape,
        in_specs=in_specs,
        out_specs=jax.tree.map(lambda _: VMEM, out_shape),
        scratch_shapes=scratch_shapes,
        compiler_params=pltpu.CompilerParams(vmem_limit_bytes=limit),
        cost_estimate=pl.CostEstimate(flops=flops, bytes_accessed=bytes_moved, transcendentals=0),
    )


def swap(blocks, bit_list, device_count):
    def position(device):
        return sum((device >> bit & 1) << rank for rank, bit in enumerate(bit_list))

    def move(device, new):
        for rank, bit in enumerate(bit_list):
            device = device & ~(1 << bit) | (new >> rank & 1) << bit
        return device

    extent = 1 << len(bit_list)
    result = []
    for parity, block in enumerate(blocks):
        route = []
        for device in range(device_count):
            at = position(device)
            partner = at + 1 if at % 2 == parity else at - 1
            if 0 <= partner < extent:
                route.append((device, move(device, partner)))
        result.append(lax.ppermute(block, "cells", route))
    return result


def local(multipoles, compress, operators, expand):
    local_bits = multipoles.shape[1].bit_length() - 1
    device_count = lax.axis_size("cells")
    bit_lists = [
        [bit for bit in range(device_count.bit_length() - 1) if (local_bits + bit) % 3 == dimension]
        for dimension in range(3)
    ]
    device = lax.axis_index("cells")
    even = jnp.stack([1 - (device >> bits[0] & 1) for bits in bit_lists]).astype(jnp.int32)

    pair = lambda count: [rows_of(count)] * 2
    tables = [
        send_table(1, Y_ROWS, TABLE),
        send_table(2, Z_ROWS, TABLE),
        window_table((1, 2)),
        window_table((0, 3)),
    ]
    table = jnp.asarray(np.concatenate(tables), BF)
    flat = operators.reshape(-1, RANK)
    own, *send = call(
        compress_kernel,
        [pltpu.VMEM((OWN, 8 * RANK), BF)] + pair(X_ROWS),
        [
            scratch(*multipoles.shape),
            scratch(*compress.shape),
            scratch(1024, RANK, kind=F32),
            scratch(2 * X_ROWS, 8 * RANK),
            pltpu.SemaphoreType.DMA((2,)),
        ],
        [SMEM] + [ANY] * 2,
    )(even, in_hbm(multipoles), in_hbm(compress))
    x_pair = swap(send, bit_lists[0], device_count)
    ops, table, token = call(
        stage_kernel,
        [
            pltpu.VMEM(flat.shape, BF),
            pltpu.VMEM(table.shape, BF),
            pltpu.VMEM((8, RANK), F32),
        ],
        [pltpu.SemaphoreType.DMA((1 + PIECES,))],
        [VMEM, ANY, ANY],
        bytes_moved=flat.size * 4,
    )(own, in_hbm(flat), in_hbm(table))
    send = call(
        forward_y_kernel,
        pair(Y_ROWS),
        [scratch(2 * X_ROWS, 8 * RANK), scratch(2 * Y_ROWS, 8 * RANK)],
        [SMEM] + [VMEM] * 5,
    )(even, own, *x_pair, table, token)
    y_pair = swap(send, bit_lists[1], device_count)
    send = call(
        forward_z_kernel,
        pair(Z_ROWS),
        [scratch(Z_BASE - OWN, 8 * RANK), scratch(2 * Z_ROWS, 8 * RANK)],
        [SMEM] + [VMEM] * 6,
    )(even, own, *x_pair, *y_pair, table)
    z_pair = swap(send, bit_lists[2], device_count)
    window = (4, 4, 2, 16, 8 * RANK)
    sums = (2, 4, 64, 2 * RANK)
    inner, partial, expand_t = call(
        inner_kernel,
        [
            pltpu.VMEM(sums, F32),
            pltpu.VMEM(window, BF),
            pltpu.VMEM(expand.shape[::-1], BF),
        ],
        [scratch(Z_BASE - OWN, 8 * RANK), scratch(*window)],
        [SMEM] + [VMEM] * 8,
        flops=5 << 30,
    )(even, own, *x_pair, *y_pair, table, expand.T, ops)
    return call(
        outer_kernel,
        jax.ShapeDtypeStruct((expand.shape[1], multipoles.shape[1]), F32),
        [
            scratch(2 * Z_ROWS, 8 * RANK),
            scratch(*window),
            scratch(*sums, kind=F32),
            scratch(1024, RANK, kind=F32),
        ],
        [SMEM] + [VMEM] * 7,
        flops=2 << 30,
    )(even, *z_pair, table, expand_t, ops, inner, partial)


def solution(mesh):
    placed = (P(None, "cells"), P(), P(), P())
    return jax.shard_map(
        local, mesh=mesh, in_specs=placed, out_specs=P(None, "cells"), check_vma=False
    )
```

```python
import functools

import jax
import jax.numpy as jnp
import numpy as np
from jax import lax
from jax.experimental import pallas as pl
from jax.experimental.pallas import tpu as pltpu
from jax.sharding import PartitionSpec as P

RANK = 128
BF = jnp.bfloat16
F32 = jnp.float32
OWN, X_ROWS, Y_ROWS, Z_ROWS = 128, 16, 48, 64
X_BASE = OWN
Y_BASE = X_BASE + 2 * X_ROWS
Z_BASE = Y_BASE + 2 * Y_ROWS
TABLE = Z_BASE + 2 * Z_ROWS
PIECES = 4
Y_TABLE, Z_TABLE, LEVEL_TABLE, SIDE_TABLE, OUTER_TABLE, ORDER_TABLE = 0, 96, 224, 480, 992, 1376

OFFSETS = [
    (dx, dy, dz)
    for dx in range(-3, 4)
    for dy in range(-3, 4)
    for dz in range(-3, 4)
    if max(abs(dx), abs(dy), abs(dz)) >= 2
]
LOOKUP = {triple: number for number, triple in enumerate(OFFSETS)}
TARGETS = [(0, 0), (0, 1), (1, 0), (1, 1)]


def table_row(bits, sub):
    (x0, y0, z0), (sx, sy, sz) = bits, sub
    xi, yi = sx + x0, sy + y0
    if sz in (-1, 2):
        return Z_BASE + (sz == 2) * Z_ROWS + (x0 + 2 * y0) * 15 + xi + 5 * yi
    if sy in (-1, 2):
        return Y_BASE + (sy == 2) * Y_ROWS + (x0 + 2 * z0) * 10 + xi + 5 * sz
    if sx in (-1, 4):
        return X_BASE + (sx == 4) * X_ROWS + (y0 + 2 * z0) * 4 + sy + 2 * sz
    return (x0 + 2 * y0 + 4 * z0) * 16 + (sx & 1) + 2 * sy + 4 * sz + 8 * (sx >> 1)


def one_hot(sources, width):
    table = np.zeros((len(sources), width), np.float32)
    for row, source in enumerate(sources):
        if source is not None:
            table[row, source] = 1.0
    return table


def send_table(dimension, rows, width):
    top = (3, 1, 1)[dimension]
    result = [None] * (2 * rows)
    base = (X_BASE, Y_BASE, Z_BASE)[dimension]
    for upward in (1, 0):
        for number in range(8):
            bits = (number & 1, number >> 1 & 1, number >> 2 & 1)
            if bits[dimension] != upward:
                continue
            ranges = [range(-b, n + 1 - b) if d < dimension else range(n) for d, (b, n) in enumerate(zip(bits, (4, 2, 2)))]
            ranges[dimension] = [top if upward else 0]
            for sx in ranges[0]:
                for sy in ranges[1]:
                    for sz in ranges[2]:
                        here = [sx, sy, sz]
                        there = list(here)
                        there[dimension] = -1 if upward else top + 1
                        landing = table_row(bits, there) - base
                        assert landing // rows == 1 - upward
                        result[landing] = table_row(bits, here)
    return one_hot(result, width)


def window_table(rows_y, planes):
    sources = []
    for px in range(4):
        for py in rows_y:
            for pz in planes:
                for column in range(16):
                    place = [2 * (column >> 2) + px - 1, (column & 3) + py - 1, pz - 1]
                    sources.append(table_row([v & 1 for v in place], [v >> 1 for v in place]))
    return one_hot(sources, TABLE)


def order_table():
    sources = []
    for parent in range(128):
        x0, y0, z0, x1, y1, z1, x2 = [parent >> bit & 1 for bit in range(7)]
        sources.append((z0 + 2 * z1) * 32 + x0 * 16 + (x1 + 2 * x2) * 4 + y0 + 2 * y1)
    return one_hot(sources, TABLE)


def matmul(a, b):
    return jnp.dot(a, b, preferred_element_type=F32)


def pick(even, sent, rows, to_even, to_odd):
    to_even[...] = sent[pl.ds(pl.multiple_of((1 - even) * rows, rows), rows), :]
    to_odd[...] = sent[pl.ds(pl.multiple_of(even * rows, rows), rows), :]


def place(even, from_even, from_odd, rows, landed):
    landed[pl.ds(pl.multiple_of(even * rows, rows), rows), :] = from_even[...]
    landed[pl.ds(pl.multiple_of((1 - even) * rows, rows), rows), :] = from_odd[...]


def x_picks():
    row = lax.broadcasted_iota(jnp.int32, (2 * X_ROWS, OWN), 0)
    column = lax.broadcasted_iota(jnp.int32, (2 * X_ROWS, OWN), 1)
    upward = 1 - (row >> 4)
    source = upward * 25 + (row >> 2 & 1) * 32 + (row >> 3 & 1) * 64 + (row & 1) * 2 + (row >> 1 & 1) * 4
    return jnp.where(column == source, 1.0, 0.0).astype(BF)


def compress_kernel(even, multipoles_hbm, compress_hbm, own, to_even, to_odd, multipoles, compress, rows, sent, sem):
    copies = [
        pltpu.make_async_copy(multipoles_hbm, multipoles, sem.at[0]),
        pltpu.make_async_copy(compress_hbm, compress, sem.at[1]),
    ]
    for copy in copies:
        copy.start()
    for copy in copies:
        copy.wait()
    rows[...] = lax.dot_general(
        multipoles[...], compress[...], (((0,), (0,)), ((), ())), preferred_element_type=F32
    )
    for number in range(8):
        for child in range(8):
            x0, y0, z0 = child & 1, child >> 1 & 1, child >> 2 & 1
            lane = ((x0 * 2 + y0) * 2 + z0) * RANK
            own[number * 16 : number * 16 + 16, lane : lane + RANK] = rows[
                pl.ds(number * 8 + child, 16, stride=64), :
            ].astype(BF)
    sent[...] = matmul(x_picks(), own[...]).astype(BF)
    pick(even[0], sent, X_ROWS, to_even, to_odd)


def stage_kernel(own, ops_hbm, table_hbm, ops, table, token, sem):
    pieces = [(table_hbm, table)]
    size = ops.shape[0] // PIECES
    for piece in range(PIECES):
        here = pl.ds(piece * size, size)
        pieces.append((ops_hbm.at[here], ops.at[here]))
    copies = [pltpu.make_async_copy(*piece, sem.at[i]) for i, piece in enumerate(pieces)]
    for copy in copies:
        copy.start()
    token[...] = jnp.zeros_like(token)
    for copy in copies:
        copy.wait()


def forward(table, own, landed, sent):
    width = OWN + landed.shape[0]
    sent[...] = (matmul(table[:, :OWN], own[...]) + matmul(table[:, OWN:width], landed[...])).astype(BF)


def forward_y_kernel(even, own, xe, xo, table, token, to_even, to_odd, landed, sent):
    place(even[0], xe, xo, X_ROWS, landed)
    forward(table.at[Y_TABLE:Z_TABLE], own, landed, sent)
    pick(even[1], sent, Y_ROWS, to_even, to_odd)


def forward_z_kernel(even, own, x_landed, yo, ye, table, token, to_even, to_odd, landed, sent):
    landed[0 : 2 * X_ROWS] = x_landed[...]
    place(even[1], ye, yo, Y_ROWS, landed.at[2 * X_ROWS :])
    forward(table.at[Z_TABLE:LEVEL_TABLE], own, landed, sent)
    pick(even[2], sent, Z_ROWS, to_even, to_odd)


def parity_shift(parity, distance):
    total = parity + distance
    return (total & 1, total >> 1) if abs(total >> 1) <= 1 else None


def operator_tiles(ops, dx, dy):
    base = LOOKUP[(dx, dy, -3)] * RANK
    if max(abs(dx), abs(dy)) >= 2:
        return [
            jnp.concatenate(
                [ops[first + RANK : first + 3 * RANK, :], ops[first : first + 2 * RANK, :]], axis=1
            )
            for first in (base, base + 2 * RANK, base + 4 * RANK)
        ]
    zero = jnp.zeros((RANK, RANK), BF)
    op = {dz: ops[base + i * RANK : base + (i + 1) * RANK, :] for i, dz in enumerate((-3, -2, 2, 3))}
    below = jnp.concatenate(
        [jnp.concatenate([op[-2], op[-3]], axis=1), jnp.concatenate([zero, op[-2]], axis=1)], axis=0
    )
    above = jnp.concatenate(
        [jnp.concatenate([op[2], zero], axis=1), jnp.concatenate([op[3], op[2]], axis=1)], axis=0
    )
    return [below, None, above]


def accumulate(source, ops, planes, pairs, targets, distances):
    total = None
    for dx, dy in distances:
        tiles = operator_tiles(ops, dx, dy)
        for pair in pairs:
            if tiles[pair] is None:
                continue
            parts = []
            for plane in planes:
                for target in targets:
                    (qx, cx), (qy, cy) = parity_shift(target[0], dx), parity_shift(target[1], dy)
                    lane = (qx * 2 + qy) * 2 * RANK
                    block = source(cx, cy, plane + pair, slice(lane, lane + 2 * RANK))
                    parts.append(block.reshape(32, 2 * RANK))
            left = jnp.concatenate(parts, axis=0) if len(parts) > 1 else parts[0]
            term = matmul(left, tiles[pair])
            total = term if total is None else total + term
    return total


def interact(source, ops, before, after, planes, pairs, shared, special):
    def add(targets, distances, start):
        total = accumulate(source, ops, planes, pairs, targets, distances)
        for i, plane in enumerate(planes):
            for j, target in enumerate(targets):
                number = TARGETS.index(target)
                first = (i * len(targets) + j) * 32
                part = total[first : first + 32]
                after[plane, number] = part if start is None else start[plane, number] + part

    near, far = range(-2, 3), (3, -3)
    add(TARGETS, [(dx, dy) for dx in near for dy in shared], before)
    for x0 in (0, 1):
        add([(x0, 0), (x0, 1)], [(far[x0], dy) for dy in shared], after)
    for y0 in (0, 1):
        add([(0, y0), (1, y0)], [(dx, dy) for dx in near for dy in special[y0]], after)
    for x0, y0 in TARGETS:
        add([(x0, y0)], [(far[x0], dy) for dy in special[y0]], after)


ALL_PLANES, ALL_PAIRS = range(4), range(3)


def fill(window, table, own, landed):
    width = OWN + landed.shape[0]
    rows = table.shape[0] // 4
    for px in range(4):
        block = table[px * rows : px * rows + rows, :width]
        filled = matmul(block[:, :OWN], own[...]) + matmul(block[:, OWN:], landed[...])
        inside = filled.astype(BF).reshape(window.shape[1], 4, 16, 8 * RANK)
        window[px, :, 1:5] = inside
        window[px, :, 0:1] = jnp.zeros_like(inside[:, :1])
        window[px, :, 5:6] = jnp.zeros_like(inside[:, :1])


def level_kernel(own, landed, table, ops, acc, token, window):
    token[...] = jnp.zeros_like(token)
    fill(window, table.at[LEVEL_TABLE:SIDE_TABLE], own, landed)

    def source(cx, cy, plane, lanes):
        return window[1 + cx : 3 + cx, 0, plane, :, lanes]

    interact(source, ops, None, acc, ALL_PLANES, ALL_PAIRS, [0], ([1], [-1]))


def side_kernel(own, landed, table, expand, ops, level, acc, expand_out, window):
    expand_out[...] = expand[...]
    fill(window, table.at[SIDE_TABLE:OUTER_TABLE], own, landed)

    def source(cx, cy, plane, lanes):
        return window[1 + cx : 3 + cx, (cy + 1) // 2, plane, :, lanes]

    interact(source, ops, level, acc, ALL_PLANES, ALL_PAIRS, [-2, 2], ([-1, 3], [-3, 1]))


def outer_kernel(even, ze, zo, table, expand, ops, inner, out, landed, window, acc, rows):
    place(even[2], ze, zo, Z_ROWS, landed)
    for px in range(4):
        block = table[OUTER_TABLE + px * 96 : OUTER_TABLE + px * 96 + 96, Z_BASE:]
        window[px] = matmul(block, landed[...]).astype(BF).reshape(window.shape[1:])

    def source(cx, cy, plane, lanes):
        return window[1 + cx : 3 + cx, 1 + cy, plane // 5, :, lanes]

    for planes, pairs in (((0,), (0,)), ((3,), (2,))):
        interact(source, ops, inner, acc, planes, pairs, range(-2, 3), ([3], [-3]))
    order = table[ORDER_TABLE : ORDER_TABLE + 128, :128]
    for number, (x0, y0) in enumerate(TARGETS):
        whole = jnp.concatenate(
            [(acc if plane in (0, 3) else inner)[plane, number].astype(BF) for plane in range(4)], axis=0
        )
        ordered = matmul(order, whole)
        for z0 in (0, 1):
            rows[pl.ds(x0 + 2 * y0 + 4 * z0, 128, stride=8), :] = ordered[:, z0 * RANK : z0 * RANK + RANK]
    out[...] = lax.dot_general(
        expand[...], rows[...].astype(BF), (((1,), (1,)), ((), ())), preferred_element_type=F32
    )


VMEM = pl.BlockSpec(memory_space=pltpu.VMEM)
ANY = pl.BlockSpec(memory_space=pl.ANY)
SMEM = pl.BlockSpec(memory_space=pltpu.SMEM)


def rows_of(count):
    return jax.ShapeDtypeStruct((count, 8 * RANK), BF)


def in_hbm(array):
    return pltpu.with_memory_space_constraint(array, pltpu.HBM)


def scratch(*shape, kind=BF):
    return pltpu.VMEM(shape, kind)


def call(kernel, out_shape, scratch_shapes, in_specs, limit=16 << 20, flops=1 << 24, bytes_moved=1 << 20):
    return pl.pallas_call(
        kernel,
        out_shape=out_shape,
        in_specs=in_specs,
        out_specs=jax.tree.map(lambda _: VMEM, out_shape),
        scratch_shapes=scratch_shapes,
        compiler_params=pltpu.CompilerParams(vmem_limit_bytes=limit),
        cost_estimate=pl.CostEstimate(flops=flops, bytes_accessed=bytes_moved, transcendentals=0),
    )


def swap(blocks, bit_list, device_count):
    def position(device):
        return sum((device >> bit & 1) << rank for rank, bit in enumerate(bit_list))

    def move(device, new):
        for rank, bit in enumerate(bit_list):
            device = device & ~(1 << bit) | (new >> rank & 1) << bit
        return device

    extent = 1 << len(bit_list)
    result = []
    for parity, block in enumerate(blocks):
        route = []
        for device in range(device_count):
            at = position(device)
            partner = at + 1 if at % 2 == parity else at - 1
            if 0 <= partner < extent:
                route.append((device, move(device, partner)))
        result.append(lax.ppermute(block, "cells", route))
    return result


def local(multipoles, compress, operators, expand):
    local_bits = multipoles.shape[1].bit_length() - 1
    device_count = lax.axis_size("cells")
    bit_lists = [
        [bit for bit in range(device_count.bit_length() - 1) if (local_bits + bit) % 3 == dimension]
        for dimension in range(3)
    ]
    device = lax.axis_index("cells")
    even = jnp.stack([1 - (device >> bits[0] & 1) for bits in bit_lists]).astype(jnp.int32)

    pair = lambda count: [rows_of(count)] * 2
    tables = [
        send_table(1, Y_ROWS, TABLE),
        send_table(2, Z_ROWS, TABLE),
        window_table((1,), range(1, 5)),
        window_table((0, 2), range(1, 5)),
        window_table(range(3), (0, 5)),
        order_table(),
    ]
    table = jnp.asarray(np.concatenate(tables), BF)
    flat = operators.reshape(-1, RANK)
    own, *send = call(
        compress_kernel,
        [pltpu.VMEM((OWN, 8 * RANK), BF)] + pair(X_ROWS),
        [
            scratch(*multipoles.shape),
            scratch(*compress.shape),
            scratch(1024, RANK, kind=F32),
            scratch(2 * X_ROWS, 8 * RANK),
            pltpu.SemaphoreType.DMA((2,)),
        ],
        [SMEM] + [ANY] * 2,
    )(even, in_hbm(multipoles), in_hbm(compress))
    x_pair = swap(send, bit_lists[0], device_count)
    ops, table, token = call(
        stage_kernel,
        [
            pltpu.VMEM(flat.shape, BF),
            pltpu.VMEM(table.shape, BF),
            pltpu.VMEM((8, RANK), F32),
        ],
        [pltpu.SemaphoreType.DMA((1 + PIECES,))],
        [VMEM, ANY, ANY],
        bytes_moved=flat.size * 4,
    )(own, in_hbm(flat), in_hbm(table))
    *send, landed = call(
        forward_y_kernel,
        pair(Y_ROWS) + [pltpu.VMEM((2 * X_ROWS, 8 * RANK), BF)],
        [scratch(2 * Y_ROWS, 8 * RANK)],
        [SMEM] + [VMEM] * 5,
    )(even, own, *x_pair, table, token)
    y_pair = swap(send, bit_lists[1], device_count)
    sums = (4, 4, 32, 2 * RANK)
    level, token = call(
        level_kernel,
        [pltpu.VMEM(sums, F32), pltpu.VMEM((8, RANK), F32)],
        [scratch(4, 1, 6, 16, 8 * RANK)],
        [VMEM] * 4,
        flops=2 << 30,
    )(own, landed, table, ops)
    *send, landed = call(
        forward_z_kernel,
        pair(Z_ROWS) + [pltpu.VMEM((Z_BASE - OWN, 8 * RANK), BF)],
        [scratch(2 * Z_ROWS, 8 * RANK)],
        [SMEM] + [VMEM] * 6,
    )(even, own, landed, *y_pair[::-1], table, token)
    z_pair = swap(send, bit_lists[2], device_count)
    inner, expand_t = call(
        side_kernel,
        [pltpu.VMEM(sums, F32), pltpu.VMEM(expand.shape[::-1], BF)],
        [scratch(4, 2, 6, 16, 8 * RANK)],
        [VMEM] * 6,
        flops=5 << 30,
    )(own, landed, table, expand.T, ops, level)
    return call(
        outer_kernel,
        jax.ShapeDtypeStruct((expand.shape[1], multipoles.shape[1]), F32),
        [
            scratch(2 * Z_ROWS, 8 * RANK),
            scratch(4, 3, 2, 16, 8 * RANK),
            scratch(*sums, kind=F32),
            scratch(1024, RANK, kind=F32),
        ],
        [SMEM] + [VMEM] * 6,
        flops=2 << 30,
    )(even, *z_pair, table, expand_t, ops, inner)


def solution(mesh):
    placed = (P(None, "cells"), P(), P(), P())
    return jax.shard_map(
        local, mesh=mesh, in_specs=placed, out_specs=P(None, "cells"), check_vma=False
    )
```

```python
import functools

import jax
import jax.numpy as jnp
import numpy as np
from jax import lax
from jax.experimental import pallas as pl
from jax.experimental.pallas import tpu as pltpu
from jax.sharding import PartitionSpec as P

RANK = 128
BF = jnp.bfloat16
F32 = jnp.float32
OWN, X_ROWS, Y_ROWS, Z_ROWS = 128, 16, 48, 64
X_BASE = OWN
Y_BASE = X_BASE + 2 * X_ROWS
Z_BASE = Y_BASE + 2 * Y_ROWS
TABLE = Z_BASE + 2 * Z_ROWS
FIRST_FLOPS = 1 << 34
Y_TABLE, Z_TABLE, LEVEL_TABLE, SIDE_TABLE, OUTER_TABLE, ORDER_TABLE = 0, 96, 224, 480, 992, 1376

OFFSETS = [
    (dx, dy, dz)
    for dx in range(-3, 4)
    for dy in range(-3, 4)
    for dz in range(-3, 4)
    if max(abs(dx), abs(dy), abs(dz)) >= 2
]
LOOKUP = {triple: number for number, triple in enumerate(OFFSETS)}
TARGETS = [(0, 0), (0, 1), (1, 0), (1, 1)]


def table_row(bits, sub):
    (x0, y0, z0), (sx, sy, sz) = bits, sub
    xi, yi = sx + x0, sy + y0
    if sz in (-1, 2):
        return Z_BASE + (sz == 2) * Z_ROWS + (x0 + 2 * y0) * 15 + xi + 5 * yi
    if sy in (-1, 2):
        return Y_BASE + (sy == 2) * Y_ROWS + (x0 + 2 * z0) * 10 + xi + 5 * sz
    if sx in (-1, 4):
        return X_BASE + (sx == 4) * X_ROWS + (y0 + 2 * z0) * 4 + sy + 2 * sz
    return (x0 + 2 * y0 + 4 * z0) * 16 + (sx & 1) + 2 * sy + 4 * sz + 8 * (sx >> 1)


def one_hot(sources, width):
    table = np.zeros((len(sources), width), np.float32)
    for row, source in enumerate(sources):
        if source is not None:
            table[row, source] = 1.0
    return table


def send_table(dimension, rows, width):
    top = (3, 1, 1)[dimension]
    result = [None] * (2 * rows)
    base = (X_BASE, Y_BASE, Z_BASE)[dimension]
    for upward in (1, 0):
        for number in range(8):
            bits = (number & 1, number >> 1 & 1, number >> 2 & 1)
            if bits[dimension] != upward:
                continue
            ranges = [range(-b, n + 1 - b) if d < dimension else range(n) for d, (b, n) in enumerate(zip(bits, (4, 2, 2)))]
            ranges[dimension] = [top if upward else 0]
            for sx in ranges[0]:
                for sy in ranges[1]:
                    for sz in ranges[2]:
                        here = [sx, sy, sz]
                        there = list(here)
                        there[dimension] = -1 if upward else top + 1
                        landing = table_row(bits, there) - base
                        assert landing // rows == 1 - upward
                        result[landing] = table_row(bits, here)
    return one_hot(result, width)


def window_table(rows_y, planes):
    sources = []
    for px in range(4):
        for py in rows_y:
            for pz in planes:
                for column in range(16):
                    place = [2 * (column >> 2) + px - 1, (column & 3) + py - 1, pz - 1]
                    sources.append(table_row([v & 1 for v in place], [v >> 1 for v in place]))
    return one_hot(sources, TABLE)


def order_table():
    sources = []
    for parent in range(128):
        x0, y0, z0, x1, y1, z1, x2 = [parent >> bit & 1 for bit in range(7)]
        sources.append((z0 + 2 * z1) * 32 + x0 * 16 + (x1 + 2 * x2) * 4 + y0 + 2 * y1)
    return one_hot(sources, TABLE)


def matmul(a, b):
    return jnp.dot(a, b, preferred_element_type=F32)


def pick(even, sent, rows, to_even, to_odd):
    to_even[...] = sent[pl.ds(pl.multiple_of((1 - even) * rows, rows), rows), :]
    to_odd[...] = sent[pl.ds(pl.multiple_of(even * rows, rows), rows), :]


def place(even, from_even, from_odd, rows, landed):
    landed[pl.ds(pl.multiple_of(even * rows, rows), rows), :] = from_even[...]
    landed[pl.ds(pl.multiple_of((1 - even) * rows, rows), rows), :] = from_odd[...]


def x_picks():
    row = lax.broadcasted_iota(jnp.int32, (2 * X_ROWS, OWN), 0)
    column = lax.broadcasted_iota(jnp.int32, (2 * X_ROWS, OWN), 1)
    upward = 1 - (row >> 4)
    source = upward * 25 + (row >> 2 & 1) * 32 + (row >> 3 & 1) * 64 + (row & 1) * 2 + (row >> 1 & 1) * 4
    return jnp.where(column == source, 1.0, 0.0).astype(BF)


def compress_kernel(even, multipoles_hbm, compress_hbm, own, to_even, to_odd, multipoles, compress, rows, sent, sem):
    copies = [
        pltpu.make_async_copy(multipoles_hbm, multipoles, sem.at[0]),
        pltpu.make_async_copy(compress_hbm, compress, sem.at[1]),
    ]
    for copy in copies:
        copy.start()
    for copy in copies:
        copy.wait()
    rows[...] = lax.dot_general(
        multipoles[...], compress[...], (((0,), (0,)), ((), ())), preferred_element_type=F32
    )
    for number in range(8):
        for child in range(8):
            x0, y0, z0 = child & 1, child >> 1 & 1, child >> 2 & 1
            lane = ((x0 * 2 + y0) * 2 + z0) * RANK
            own[number * 16 : number * 16 + 16, lane : lane + RANK] = rows[
                pl.ds(number * 8 + child, 16, stride=64), :
            ].astype(BF)
    sent[...] = matmul(x_picks(), own[...]).astype(BF)
    pick(even[0], sent, X_ROWS, to_even, to_odd)


def forward(table, own, landed, sent):
    width = OWN + landed.shape[0]
    sent[...] = (matmul(table[:, :OWN], own[...]) + matmul(table[:, OWN:width], landed[...])).astype(BF)


def forward_y_kernel(even, own, xe, xo, table, to_even, to_odd, landed, sent):
    place(even[0], xe, xo, X_ROWS, landed)
    forward(table.at[Y_TABLE:Z_TABLE], own, landed, sent)
    pick(even[1], sent, Y_ROWS, to_even, to_odd)


def forward_z_kernel(even, own, x_landed, yo, ye, table, token, to_even, to_odd, landed, sent):
    landed[0 : 2 * X_ROWS] = x_landed[...]
    place(even[1], ye, yo, Y_ROWS, landed.at[2 * X_ROWS :])
    forward(table.at[Z_TABLE:LEVEL_TABLE], own, landed, sent)
    pick(even[2], sent, Z_ROWS, to_even, to_odd)


def parity_shift(parity, distance):
    total = parity + distance
    return (total & 1, total >> 1) if abs(total >> 1) <= 1 else None


def operator_tiles(ops, dx, dy):
    base = LOOKUP[(dx, dy, -3)] * RANK
    if max(abs(dx), abs(dy)) >= 2:
        return [
            jnp.concatenate(
                [ops[first + RANK : first + 3 * RANK, :], ops[first : first + 2 * RANK, :]], axis=1
            )
            for first in (base, base + 2 * RANK, base + 4 * RANK)
        ]
    zero = jnp.zeros((RANK, RANK), BF)
    op = {dz: ops[base + i * RANK : base + (i + 1) * RANK, :] for i, dz in enumerate((-3, -2, 2, 3))}
    below = jnp.concatenate(
        [jnp.concatenate([op[-2], op[-3]], axis=1), jnp.concatenate([zero, op[-2]], axis=1)], axis=0
    )
    above = jnp.concatenate(
        [jnp.concatenate([op[2], zero], axis=1), jnp.concatenate([op[3], op[2]], axis=1)], axis=0
    )
    return [below, None, above]


def accumulate(source, ops, planes, pairs, targets, distances):
    total = None
    for dx, dy in distances:
        tiles = operator_tiles(ops, dx, dy)
        for pair in pairs:
            if tiles[pair] is None:
                continue
            parts = []
            for plane in planes:
                for target in targets:
                    (qx, cx), (qy, cy) = parity_shift(target[0], dx), parity_shift(target[1], dy)
                    lane = (qx * 2 + qy) * 2 * RANK
                    block = source(cx, cy, plane + pair, slice(lane, lane + 2 * RANK))
                    parts.append(block.reshape(32, 2 * RANK))
            left = jnp.concatenate(parts, axis=0) if len(parts) > 1 else parts[0]
            term = matmul(left, tiles[pair])
            total = term if total is None else total + term
    return total


def interact(source, ops, before, after, planes, pairs, shared, special):
    def add(targets, distances, start):
        total = accumulate(source, ops, planes, pairs, targets, distances)
        for i, plane in enumerate(planes):
            for j, target in enumerate(targets):
                number = TARGETS.index(target)
                first = (i * len(targets) + j) * 32
                part = total[first : first + 32]
                after[plane, number] = part if start is None else start[plane, number] + part

    near, far = range(-2, 3), (3, -3)
    add(TARGETS, [(dx, dy) for dx in near for dy in shared], before)
    for x0 in (0, 1):
        add([(x0, 0), (x0, 1)], [(far[x0], dy) for dy in shared], after)
    for y0 in (0, 1):
        add([(0, y0), (1, y0)], [(dx, dy) for dx in near for dy in special[y0]], after)
    for x0, y0 in TARGETS:
        add([(x0, y0)], [(far[x0], dy) for dy in special[y0]], after)


ALL_PLANES, ALL_PAIRS = range(4), range(3)


def fill(window, table, own, landed):
    width = OWN + landed.shape[0]
    rows = table.shape[0] // 4
    for px in range(4):
        block = table[px * rows : px * rows + rows, :width]
        filled = matmul(block[:, :OWN], own[...]) + matmul(block[:, OWN:], landed[...])
        inside = filled.astype(BF).reshape(window.shape[1], 4, 16, 8 * RANK)
        window[px, :, 1:5] = inside
        window[px, :, 0:1] = jnp.zeros_like(inside[:, :1])
        window[px, :, 5:6] = jnp.zeros_like(inside[:, :1])


def level_kernel(own, landed, table, ops, acc, token, window):
    token[...] = jnp.zeros_like(token)
    fill(window, table.at[LEVEL_TABLE:SIDE_TABLE], own, landed)

    def source(cx, cy, plane, lanes):
        return window[1 + cx : 3 + cx, 0, plane, :, lanes]

    interact(source, ops, None, acc, ALL_PLANES, ALL_PAIRS, [0], ([1], [-1]))


def side_kernel(own, landed, table, expand, ops, level, acc, expand_out, window):
    expand_out[...] = expand[...]
    fill(window, table.at[SIDE_TABLE:OUTER_TABLE], own, landed)

    def source(cx, cy, plane, lanes):
        return window[1 + cx : 3 + cx, (cy + 1) // 2, plane, :, lanes]

    interact(source, ops, level, acc, ALL_PLANES, ALL_PAIRS, [-2, 2], ([-1, 3], [-3, 1]))


def outer_kernel(even, ze, zo, table, expand, ops, inner, out, landed, window, acc, rows):
    place(even[2], ze, zo, Z_ROWS, landed)
    for px in range(4):
        block = table[OUTER_TABLE + px * 96 : OUTER_TABLE + px * 96 + 96, Z_BASE:]
        window[px] = matmul(block, landed[...]).astype(BF).reshape(window.shape[1:])

    def source(cx, cy, plane, lanes):
        return window[1 + cx : 3 + cx, 1 + cy, plane // 5, :, lanes]

    for planes, pairs in (((0,), (0,)), ((3,), (2,))):
        interact(source, ops, inner, acc, planes, pairs, range(-2, 3), ([3], [-3]))
    order = table[ORDER_TABLE : ORDER_TABLE + 128, :128]
    for number, (x0, y0) in enumerate(TARGETS):
        whole = jnp.concatenate(
            [(acc if plane in (0, 3) else inner)[plane, number].astype(BF) for plane in range(4)], axis=0
        )
        ordered = matmul(order, whole)
        for z0 in (0, 1):
            rows[pl.ds(x0 + 2 * y0 + 4 * z0, 128, stride=8), :] = ordered[:, z0 * RANK : z0 * RANK + RANK]
    out[...] = lax.dot_general(
        expand[...], rows[...].astype(BF), (((1,), (1,)), ((), ())), preferred_element_type=F32
    )


VMEM = pl.BlockSpec(memory_space=pltpu.VMEM)
ANY = pl.BlockSpec(memory_space=pl.ANY)
SMEM = pl.BlockSpec(memory_space=pltpu.SMEM)


def rows_of(count):
    return jax.ShapeDtypeStruct((count, 8 * RANK), BF)


def in_hbm(array):
    return pltpu.with_memory_space_constraint(array, pltpu.HBM)


def scratch(*shape, kind=BF):
    return pltpu.VMEM(shape, kind)


def call(kernel, out_shape, scratch_shapes, in_specs, limit=16 << 20, flops=1 << 24, bytes_moved=1 << 20):
    return pl.pallas_call(
        kernel,
        out_shape=out_shape,
        in_specs=in_specs,
        out_specs=jax.tree.map(lambda _: VMEM, out_shape),
        scratch_shapes=scratch_shapes,
        compiler_params=pltpu.CompilerParams(vmem_limit_bytes=limit),
        cost_estimate=pl.CostEstimate(flops=flops, bytes_accessed=bytes_moved, transcendentals=0),
    )


def swap(blocks, bit_list, device_count):
    def position(device):
        return sum((device >> bit & 1) << rank for rank, bit in enumerate(bit_list))

    def move(device, new):
        for rank, bit in enumerate(bit_list):
            device = device & ~(1 << bit) | (new >> rank & 1) << bit
        return device

    extent = 1 << len(bit_list)
    result = []
    for parity, block in enumerate(blocks):
        route = []
        for device in range(device_count):
            at = position(device)
            partner = at + 1 if at % 2 == parity else at - 1
            if 0 <= partner < extent:
                route.append((device, move(device, partner)))
        result.append(lax.ppermute(block, "cells", route))
    return result


def local(multipoles, compress, operators, expand):
    local_bits = multipoles.shape[1].bit_length() - 1
    device_count = lax.axis_size("cells")
    bit_lists = [
        [bit for bit in range(device_count.bit_length() - 1) if (local_bits + bit) % 3 == dimension]
        for dimension in range(3)
    ]
    device = lax.axis_index("cells")
    even = jnp.stack([1 - (device >> bits[0] & 1) for bits in bit_lists]).astype(jnp.int32)

    pair = lambda count: [rows_of(count)] * 2
    tables = [
        send_table(1, Y_ROWS, TABLE),
        send_table(2, Z_ROWS, TABLE),
        window_table((1,), range(1, 5)),
        window_table((0, 2), range(1, 5)),
        window_table(range(3), (0, 5)),
        order_table(),
    ]
    table = jnp.asarray(np.concatenate(tables), BF)
    flat = operators.reshape(-1, RANK)
    own, *send = call(
        compress_kernel,
        [pltpu.VMEM((OWN, 8 * RANK), BF)] + pair(X_ROWS),
        [
            scratch(*multipoles.shape),
            scratch(*compress.shape),
            scratch(1024, RANK, kind=F32),
            scratch(2 * X_ROWS, 8 * RANK),
            pltpu.SemaphoreType.DMA((2,)),
        ],
        [SMEM] + [ANY] * 2,
        flops=FIRST_FLOPS,
    )(even, in_hbm(multipoles), in_hbm(compress))
    x_pair = swap(send, bit_lists[0], device_count)
    ops = flat
    *send, landed = call(
        forward_y_kernel,
        pair(Y_ROWS) + [pltpu.VMEM((2 * X_ROWS, 8 * RANK), BF)],
        [scratch(2 * Y_ROWS, 8 * RANK)],
        [SMEM] + [VMEM] * 4,
    )(even, own, *x_pair, table)
    y_pair = swap(send, bit_lists[1], device_count)
    sums = (4, 4, 32, 2 * RANK)
    level, token = call(
        level_kernel,
        [pltpu.VMEM(sums, F32), pltpu.VMEM((8, RANK), F32)],
        [scratch(4, 1, 6, 16, 8 * RANK)],
        [VMEM] * 4,
        flops=2 << 30,
    )(own, landed, table, ops)
    *send, landed = call(
        forward_z_kernel,
        pair(Z_ROWS) + [pltpu.VMEM((Z_BASE - OWN, 8 * RANK), BF)],
        [scratch(2 * Z_ROWS, 8 * RANK)],
        [SMEM] + [VMEM] * 6,
    )(even, own, landed, *y_pair[::-1], table, token)
    z_pair = swap(send, bit_lists[2], device_count)
    inner, expand_t = call(
        side_kernel,
        [pltpu.VMEM(sums, F32), pltpu.VMEM(expand.shape[::-1], BF)],
        [scratch(4, 2, 6, 16, 8 * RANK)],
        [VMEM] * 6,
        flops=5 << 30,
    )(own, landed, table, expand.T, ops, level)
    return call(
        outer_kernel,
        jax.ShapeDtypeStruct((expand.shape[1], multipoles.shape[1]), F32),
        [
            scratch(2 * Z_ROWS, 8 * RANK),
            scratch(4, 3, 2, 16, 8 * RANK),
            scratch(*sums, kind=F32),
            scratch(1024, RANK, kind=F32),
        ],
        [SMEM] + [VMEM] * 6,
        flops=2 << 30,
    )(even, *z_pair, table, expand_t, ops, inner)


def solution(mesh):
    placed = (P(None, "cells"), P(), P(), P())
    return jax.shard_map(
        local, mesh=mesh, in_specs=placed, out_specs=P(None, "cells"), check_vma=False
    )
```

```python
import functools

import jax
import jax.numpy as jnp
import numpy as np
from jax import lax
from jax.experimental import pallas as pl
from jax.experimental.pallas import tpu as pltpu
from jax.sharding import PartitionSpec as P

RANK = 128
BF = jnp.bfloat16
F32 = jnp.float32
OWN, X_ROWS, Y_ROWS, Z_ROWS = 128, 16, 48, 64
X_BASE = OWN
Y_BASE = X_BASE + 2 * X_ROWS
Z_BASE = Y_BASE + 2 * Y_ROWS
TABLE = Z_BASE + 2 * Z_ROWS
FIRST_FLOPS = 1 << 34
Y_TABLE, Z_TABLE, LEVEL_TABLE, SIDE_TABLE, OUTER_TABLE, ORDER_TABLE = 0, 96, 224, 480, 992, 1376

OFFSETS = [
    (dx, dy, dz)
    for dx in range(-3, 4)
    for dy in range(-3, 4)
    for dz in range(-3, 4)
    if max(abs(dx), abs(dy), abs(dz)) >= 2
]
LOOKUP = {triple: number for number, triple in enumerate(OFFSETS)}
TARGETS = [(0, 0), (0, 1), (1, 0), (1, 1)]


def table_row(bits, sub):
    (x0, y0, z0), (sx, sy, sz) = bits, sub
    xi, yi = sx + x0, sy + y0
    if sz in (-1, 2):
        return Z_BASE + (sz == 2) * Z_ROWS + (x0 + 2 * y0) * 15 + xi + 5 * yi
    if sy in (-1, 2):
        return Y_BASE + (sy == 2) * Y_ROWS + (x0 + 2 * z0) * 10 + xi + 5 * sz
    if sx in (-1, 4):
        return X_BASE + (sx == 4) * X_ROWS + (y0 + 2 * z0) * 4 + sy + 2 * sz
    return (x0 + 2 * y0 + 4 * z0) * 16 + (sx & 1) + 2 * sy + 4 * sz + 8 * (sx >> 1)


def one_hot(sources, width):
    table = np.zeros((len(sources), width), np.float32)
    for row, source in enumerate(sources):
        if source is not None:
            table[row, source] = 1.0
    return table


def send_table(dimension, rows, width):
    top = (3, 1, 1)[dimension]
    result = [None] * (2 * rows)
    base = (X_BASE, Y_BASE, Z_BASE)[dimension]
    for upward in (1, 0):
        for number in range(8):
            bits = (number & 1, number >> 1 & 1, number >> 2 & 1)
            if bits[dimension] != upward:
                continue
            ranges = [range(-b, n + 1 - b) if d < dimension else range(n) for d, (b, n) in enumerate(zip(bits, (4, 2, 2)))]
            ranges[dimension] = [top if upward else 0]
            for sx in ranges[0]:
                for sy in ranges[1]:
                    for sz in ranges[2]:
                        here = [sx, sy, sz]
                        there = list(here)
                        there[dimension] = -1 if upward else top + 1
                        landing = table_row(bits, there) - base
                        assert landing // rows == 1 - upward
                        result[landing] = table_row(bits, here)
    return one_hot(result, width)


def window_table(rows_y, planes):
    sources = []
    for px in range(4):
        for py in rows_y:
            for pz in planes:
                for column in range(16):
                    place = [2 * (column >> 2) + px - 1, (column & 3) + py - 1, pz - 1]
                    sources.append(table_row([v & 1 for v in place], [v >> 1 for v in place]))
    return one_hot(sources, TABLE)


def order_table():
    sources = []
    for parent in range(128):
        x0, y0, z0, x1, y1, z1, x2 = [parent >> bit & 1 for bit in range(7)]
        sources.append((z0 + 2 * z1) * 32 + x0 * 16 + (x1 + 2 * x2) * 4 + y0 + 2 * y1)
    return one_hot(sources, TABLE)


def matmul(a, b):
    return jnp.dot(a, b, preferred_element_type=F32)


def pick(even, sent, rows, to_even, to_odd):
    to_even[...] = sent[pl.ds(pl.multiple_of((1 - even) * rows, rows), rows), :]
    to_odd[...] = sent[pl.ds(pl.multiple_of(even * rows, rows), rows), :]


def place(even, from_even, from_odd, rows, landed):
    landed[pl.ds(pl.multiple_of(even * rows, rows), rows), :] = from_even[...]
    landed[pl.ds(pl.multiple_of((1 - even) * rows, rows), rows), :] = from_odd[...]


def x_picks():
    row = lax.broadcasted_iota(jnp.int32, (2 * X_ROWS, OWN), 0)
    column = lax.broadcasted_iota(jnp.int32, (2 * X_ROWS, OWN), 1)
    upward = 1 - (row >> 4)
    source = upward * 25 + (row >> 2 & 1) * 32 + (row >> 3 & 1) * 64 + (row & 1) * 2 + (row >> 1 & 1) * 4
    return jnp.where(column == source, 1.0, 0.0).astype(BF)


def compress_kernel(even, multipoles_hbm, compress_hbm, own, to_even, to_odd, multipoles, compress, rows, sent, sem):
    copies = [
        pltpu.make_async_copy(multipoles_hbm, multipoles, sem.at[0]),
        pltpu.make_async_copy(compress_hbm, compress, sem.at[1]),
    ]
    for copy in copies:
        copy.start()
    for copy in copies:
        copy.wait()
    rows[...] = lax.dot_general(
        multipoles[...], compress[...], (((0,), (0,)), ((), ())), preferred_element_type=F32
    )
    for number in range(8):
        for child in range(8):
            x0, y0, z0 = child & 1, child >> 1 & 1, child >> 2 & 1
            lane = ((x0 * 2 + y0) * 2 + z0) * RANK
            own[number * 16 : number * 16 + 16, lane : lane + RANK] = rows[
                pl.ds(number * 8 + child, 16, stride=64), :
            ].astype(BF)
    sent[...] = matmul(x_picks(), own[...]).astype(BF)
    pick(even[0], sent, X_ROWS, to_even, to_odd)


def forward(table, own, landed, sent):
    width = OWN + landed.shape[0]
    sent[...] = (matmul(table[:, :OWN], own[...]) + matmul(table[:, OWN:width], landed[...])).astype(BF)


def forward_y_kernel(even, own, xo, xe, table, to_even, to_odd, landed, sent):
    place(even[0], xe, xo, X_ROWS, landed)
    forward(table.at[Y_TABLE:Z_TABLE], own, landed, sent)
    pick(even[1], sent, Y_ROWS, to_even, to_odd)


def forward_z_kernel(even, own, x_landed, yo, ye, table, token, to_even, to_odd, landed, sent):
    landed[0 : 2 * X_ROWS] = x_landed[...]
    place(even[1], ye, yo, Y_ROWS, landed.at[2 * X_ROWS :])
    forward(table.at[Z_TABLE:LEVEL_TABLE], own, landed, sent)
    pick(even[2], sent, Z_ROWS, to_even, to_odd)


def parity_shift(parity, distance):
    total = parity + distance
    return (total & 1, total >> 1) if abs(total >> 1) <= 1 else None


def operator_tiles(ops, dx, dy):
    base = LOOKUP[(dx, dy, -3)] * RANK
    if max(abs(dx), abs(dy)) >= 2:
        return [
            jnp.concatenate(
                [ops[first + RANK : first + 3 * RANK, :], ops[first : first + 2 * RANK, :]], axis=1
            )
            for first in (base, base + 2 * RANK, base + 4 * RANK)
        ]
    zero = jnp.zeros((RANK, RANK), BF)
    op = {dz: ops[base + i * RANK : base + (i + 1) * RANK, :] for i, dz in enumerate((-3, -2, 2, 3))}
    below = jnp.concatenate(
        [jnp.concatenate([op[-2], op[-3]], axis=1), jnp.concatenate([zero, op[-2]], axis=1)], axis=0
    )
    above = jnp.concatenate(
        [jnp.concatenate([op[2], zero], axis=1), jnp.concatenate([op[3], op[2]], axis=1)], axis=0
    )
    return [below, None, above]


def accumulate(source, ops, planes, pairs, targets, distances):
    total = None
    for dx, dy in distances:
        tiles = operator_tiles(ops, dx, dy)
        for pair in pairs:
            if tiles[pair] is None:
                continue
            parts = []
            for plane in planes:
                for target in targets:
                    (qx, cx), (qy, cy) = parity_shift(target[0], dx), parity_shift(target[1], dy)
                    lane = (qx * 2 + qy) * 2 * RANK
                    block = source(cx, cy, plane + pair, slice(lane, lane + 2 * RANK))
                    parts.append(block.reshape(32, 2 * RANK))
            left = jnp.concatenate(parts, axis=0) if len(parts) > 1 else parts[0]
            term = matmul(left, tiles[pair])
            total = term if total is None else total + term
    return total


def interact(source, ops, before, after, planes, pairs, shared, special):
    def add(targets, distances, start):
        total = accumulate(source, ops, planes, pairs, targets, distances)
        for i, plane in enumerate(planes):
            for j, target in enumerate(targets):
                number = TARGETS.index(target)
                first = (i * len(targets) + j) * 32
                part = total[first : first + 32]
                after[plane, number] = part if start is None else start[plane, number] + part

    near, far = range(-2, 3), (3, -3)
    add(TARGETS, [(dx, dy) for dx in near for dy in shared], before)
    for x0 in (0, 1):
        add([(x0, 0), (x0, 1)], [(far[x0], dy) for dy in shared], after)
    for y0 in (0, 1):
        add([(0, y0), (1, y0)], [(dx, dy) for dx in near for dy in special[y0]], after)
    for x0, y0 in TARGETS:
        add([(x0, y0)], [(far[x0], dy) for dy in special[y0]], after)


ALL_PLANES, ALL_PAIRS = range(4), range(3)


def fill(window, table, own, landed):
    width = OWN + landed.shape[0]
    rows = table.shape[0] // 4
    for px in range(4):
        block = table[px * rows : px * rows + rows, :width]
        filled = matmul(block[:, :OWN], own[...]) + matmul(block[:, OWN:], landed[...])
        inside = filled.astype(BF).reshape(window.shape[1], 4, 16, 8 * RANK)
        window[px, :, 1:5] = inside
        window[px, :, 0:1] = jnp.zeros_like(inside[:, :1])
        window[px, :, 5:6] = jnp.zeros_like(inside[:, :1])


def level_kernel(own, landed, table, ops, acc, token, window):
    token[...] = jnp.zeros_like(token)
    fill(window, table.at[LEVEL_TABLE:SIDE_TABLE], own, landed)

    def source(cx, cy, plane, lanes):
        return window[1 + cx : 3 + cx, 0, plane, :, lanes]

    interact(source, ops, None, acc, ALL_PLANES, ALL_PAIRS, [0], ([1], [-1]))


def side_kernel(own, landed, table, expand, ops, level, acc, expand_out, window):
    expand_out[...] = expand[...]
    fill(window, table.at[SIDE_TABLE:OUTER_TABLE], own, landed)

    def source(cx, cy, plane, lanes):
        return window[1 + cx : 3 + cx, (cy + 1) // 2, plane, :, lanes]

    interact(source, ops, level, acc, ALL_PLANES, ALL_PAIRS, [-2, 2], ([-1, 3], [-3, 1]))


def outer_kernel(even, ze, zo, table, expand, ops, inner, out, landed, window, acc, rows):
    place(even[2], ze, zo, Z_ROWS, landed)
    for px in range(4):
        block = table[OUTER_TABLE + px * 96 : OUTER_TABLE + px * 96 + 96, Z_BASE:]
        window[px] = matmul(block, landed[...]).astype(BF).reshape(window.shape[1:])

    def source(cx, cy, plane, lanes):
        return window[1 + cx : 3 + cx, 1 + cy, plane // 5, :, lanes]

    for planes, pairs in (((0,), (0,)), ((3,), (2,))):
        interact(source, ops, inner, acc, planes, pairs, range(-2, 3), ([3], [-3]))
    order = table[ORDER_TABLE : ORDER_TABLE + 128, :128]
    for number, (x0, y0) in enumerate(TARGETS):
        whole = jnp.concatenate(
            [(acc if plane in (0, 3) else inner)[plane, number].astype(BF) for plane in range(4)], axis=0
        )
        ordered = matmul(order, whole)
        for z0 in (0, 1):
            rows[pl.ds(x0 + 2 * y0 + 4 * z0, 128, stride=8), :] = ordered[:, z0 * RANK : z0 * RANK + RANK]
    out[...] = lax.dot_general(
        expand[...], rows[...].astype(BF), (((1,), (1,)), ((), ())), preferred_element_type=F32
    )


VMEM = pl.BlockSpec(memory_space=pltpu.VMEM)
ANY = pl.BlockSpec(memory_space=pl.ANY)
SMEM = pl.BlockSpec(memory_space=pltpu.SMEM)


def rows_of(count):
    return jax.ShapeDtypeStruct((count, 8 * RANK), BF)


def in_hbm(array):
    return pltpu.with_memory_space_constraint(array, pltpu.HBM)


def scratch(*shape, kind=BF):
    return pltpu.VMEM(shape, kind)


def call(kernel, out_shape, scratch_shapes, in_specs, limit=16 << 20, flops=1 << 24, bytes_moved=1 << 20):
    return pl.pallas_call(
        kernel,
        out_shape=out_shape,
        in_specs=in_specs,
        out_specs=jax.tree.map(lambda _: VMEM, out_shape),
        scratch_shapes=scratch_shapes,
        compiler_params=pltpu.CompilerParams(vmem_limit_bytes=limit),
        cost_estimate=pl.CostEstimate(flops=flops, bytes_accessed=bytes_moved, transcendentals=0),
    )


def swap(blocks, bit_list, device_count):
    def position(device):
        return sum((device >> bit & 1) << rank for rank, bit in enumerate(bit_list))

    def move(device, new):
        for rank, bit in enumerate(bit_list):
            device = device & ~(1 << bit) | (new >> rank & 1) << bit
        return device

    extent = 1 << len(bit_list)
    result = []
    for parity, block in enumerate(blocks):
        route = []
        for device in range(device_count):
            at = position(device)
            partner = at + 1 if at % 2 == parity else at - 1
            if 0 <= partner < extent:
                route.append((device, move(device, partner)))
        result.append(lax.ppermute(block, "cells", route))
    return result


def local(multipoles, compress, operators, expand):
    local_bits = multipoles.shape[1].bit_length() - 1
    device_count = lax.axis_size("cells")
    bit_lists = [
        [bit for bit in range(device_count.bit_length() - 1) if (local_bits + bit) % 3 == dimension]
        for dimension in range(3)
    ]
    device = lax.axis_index("cells")
    even = jnp.stack([1 - (device >> bits[0] & 1) for bits in bit_lists]).astype(jnp.int32)

    pair = lambda count: [rows_of(count)] * 2
    tables = [
        send_table(1, Y_ROWS, TABLE),
        send_table(2, Z_ROWS, TABLE),
        window_table((1,), range(1, 5)),
        window_table((0, 2), range(1, 5)),
        window_table(range(3), (0, 5)),
        order_table(),
    ]
    table = jnp.asarray(np.concatenate(tables), BF)
    flat = operators.reshape(-1, RANK)
    own, *send = call(
        compress_kernel,
        [pltpu.VMEM((OWN, 8 * RANK), BF)] + pair(X_ROWS),
        [
            scratch(*multipoles.shape),
            scratch(*compress.shape),
            scratch(1024, RANK, kind=F32),
            scratch(2 * X_ROWS, 8 * RANK),
            pltpu.SemaphoreType.DMA((2,)),
        ],
        [SMEM] + [ANY] * 2,
        flops=FIRST_FLOPS,
    )(even, in_hbm(multipoles), in_hbm(compress))
    x_pair = swap(send, bit_lists[0], device_count)
    ops = flat
    *send, landed = call(
        forward_y_kernel,
        pair(Y_ROWS) + [pltpu.VMEM((2 * X_ROWS, 8 * RANK), BF)],
        [scratch(2 * Y_ROWS, 8 * RANK)],
        [SMEM] + [VMEM] * 4,
    )(even, own, *x_pair[::-1], table)
    y_pair = swap(send, bit_lists[1], device_count)
    sums = (4, 4, 32, 2 * RANK)
    level, token = call(
        level_kernel,
        [pltpu.VMEM(sums, F32), pltpu.VMEM((8, RANK), F32)],
        [scratch(4, 1, 6, 16, 8 * RANK)],
        [VMEM] * 4,
        flops=2 << 30,
    )(own, landed, table, ops)
    *send, landed = call(
        forward_z_kernel,
        pair(Z_ROWS) + [pltpu.VMEM((Z_BASE - OWN, 8 * RANK), BF)],
        [scratch(2 * Z_ROWS, 8 * RANK)],
        [SMEM] + [VMEM] * 6,
    )(even, own, landed, *y_pair[::-1], table, token)
    z_pair = swap(send, bit_lists[2], device_count)
    inner, expand_t = call(
        side_kernel,
        [pltpu.VMEM(sums, F32), pltpu.VMEM(expand.shape[::-1], BF)],
        [scratch(4, 2, 6, 16, 8 * RANK)],
        [VMEM] * 6,
        flops=5 << 30,
    )(own, landed, table, expand.T, ops, level)
    return call(
        outer_kernel,
        jax.ShapeDtypeStruct((expand.shape[1], multipoles.shape[1]), F32),
        [
            scratch(2 * Z_ROWS, 8 * RANK),
            scratch(4, 3, 2, 16, 8 * RANK),
            scratch(*sums, kind=F32),
            scratch(1024, RANK, kind=F32),
        ],
        [SMEM] + [VMEM] * 6,
        flops=2 << 30,
    )(even, *z_pair, table, expand_t, ops, inner)


def solution(mesh):
    placed = (P(None, "cells"), P(), P(), P())
    return jax.shard_map(
        local, mesh=mesh, in_specs=placed, out_specs=P(None, "cells"), check_vma=False
    )
```

```python
import functools

import jax
import jax.numpy as jnp
import numpy as np
from jax import lax
from jax.experimental import pallas as pl
from jax.experimental.pallas import tpu as pltpu
from jax.sharding import PartitionSpec as P

RANK = 128
BF = jnp.bfloat16
F32 = jnp.float32
OWN, X_ROWS, Y_ROWS, Z_ROWS = 128, 16, 48, 64
X_BASE = OWN
Y_BASE = X_BASE + 2 * X_ROWS
Z_BASE = Y_BASE + 2 * Y_ROWS
TABLE = Z_BASE + 2 * Z_ROWS
FIRST_FLOPS = 1 << 34
Y_TABLE, Z_TABLE, LEVEL_TABLE, SIDE_TABLE, OUTER_TABLE, ORDER_TABLE = 0, 96, 224, 480, 992, 1376

OFFSETS = [
    (dx, dy, dz)
    for dx in range(-3, 4)
    for dy in range(-3, 4)
    for dz in range(-3, 4)
    if max(abs(dx), abs(dy), abs(dz)) >= 2
]
LOOKUP = {triple: number for number, triple in enumerate(OFFSETS)}
TARGETS = [(0, 0), (0, 1), (1, 0), (1, 1)]


def table_row(bits, sub):
    (x0, y0, z0), (sx, sy, sz) = bits, sub
    xi, yi = sx + x0, sy + y0
    if sz in (-1, 2):
        return Z_BASE + (sz == 2) * Z_ROWS + (x0 + 2 * y0) * 15 + xi + 5 * yi
    if sy in (-1, 2):
        return Y_BASE + (sy == 2) * Y_ROWS + (x0 + 2 * z0) * 10 + xi + 5 * sz
    if sx in (-1, 4):
        return X_BASE + (sx == 4) * X_ROWS + (y0 + 2 * z0) * 4 + sy + 2 * sz
    return (x0 + 2 * y0 + 4 * z0) * 16 + (sx & 1) + 2 * sy + 4 * sz + 8 * (sx >> 1)


def one_hot(sources, width):
    table = np.zeros((len(sources), width), np.float32)
    for row, source in enumerate(sources):
        if source is not None:
            table[row, source] = 1.0
    return table


def send_table(dimension, rows, width):
    top = (3, 1, 1)[dimension]
    result = [None] * (2 * rows)
    base = (X_BASE, Y_BASE, Z_BASE)[dimension]
    for upward in (1, 0):
        for number in range(8):
            bits = (number & 1, number >> 1 & 1, number >> 2 & 1)
            if bits[dimension] != upward:
                continue
            ranges = [range(-b, n + 1 - b) if d < dimension else range(n) for d, (b, n) in enumerate(zip(bits, (4, 2, 2)))]
            ranges[dimension] = [top if upward else 0]
            for sx in ranges[0]:
                for sy in ranges[1]:
                    for sz in ranges[2]:
                        here = [sx, sy, sz]
                        there = list(here)
                        there[dimension] = -1 if upward else top + 1
                        landing = table_row(bits, there) - base
                        assert landing // rows == 1 - upward
                        result[landing] = table_row(bits, here)
    return one_hot(result, width)


def window_table(rows_y, planes):
    sources = []
    for px in range(4):
        for py in rows_y:
            for pz in planes:
                for column in range(16):
                    place = [2 * (column >> 2) + px - 1, (column & 3) + py - 1, pz - 1]
                    sources.append(table_row([v & 1 for v in place], [v >> 1 for v in place]))
    return one_hot(sources, TABLE)


def order_table():
    sources = []
    for parent in range(128):
        x0, y0, z0, x1, y1, z1, x2 = [parent >> bit & 1 for bit in range(7)]
        sources.append((z0 + 2 * z1) * 32 + x0 * 16 + (x1 + 2 * x2) * 4 + y0 + 2 * y1)
    return one_hot(sources, TABLE)


def matmul(a, b):
    return jnp.dot(a, b, preferred_element_type=F32)


def pick(even, sent, rows, to_even, to_odd):
    to_even[...] = sent[pl.ds(pl.multiple_of((1 - even) * rows, rows), rows), :]
    to_odd[...] = sent[pl.ds(pl.multiple_of(even * rows, rows), rows), :]


def place(even, from_even, from_odd, rows, landed):
    landed[pl.ds(pl.multiple_of(even * rows, rows), rows), :] = from_even[...]
    landed[pl.ds(pl.multiple_of((1 - even) * rows, rows), rows), :] = from_odd[...]


def x_picks():
    row = lax.broadcasted_iota(jnp.int32, (2 * X_ROWS, OWN), 0)
    column = lax.broadcasted_iota(jnp.int32, (2 * X_ROWS, OWN), 1)
    upward = 1 - (row >> 4)
    source = upward * 25 + (row >> 2 & 1) * 32 + (row >> 3 & 1) * 64 + (row & 1) * 2 + (row >> 1 & 1) * 4
    return jnp.where(column == source, 1.0, 0.0).astype(BF)


def compress_kernel(even, multipoles_hbm, compress_hbm, own, to_even, to_odd, multipoles, compress, rows, sent, sem):
    copies = [
        pltpu.make_async_copy(multipoles_hbm, multipoles, sem.at[0]),
        pltpu.make_async_copy(compress_hbm, compress, sem.at[1]),
    ]
    for copy in copies:
        copy.start()
    for copy in copies:
        copy.wait()
    rows[...] = lax.dot_general(
        multipoles[...], compress[...], (((0,), (0,)), ((), ())), preferred_element_type=F32
    )
    for number in range(8):
        for child in range(8):
            x0, y0, z0 = child & 1, child >> 1 & 1, child >> 2 & 1
            lane = ((x0 * 2 + y0) * 2 + z0) * RANK
            own[number * 16 : number * 16 + 16, lane : lane + RANK] = rows[
                pl.ds(number * 8 + child, 16, stride=64), :
            ].astype(BF)
    sent[...] = matmul(x_picks(), own[...]).astype(BF)
    pick(even[0], sent, X_ROWS, to_even, to_odd)


def forward(table, own, landed, sent):
    width = OWN + landed.shape[0]
    sent[...] = (matmul(table[:, :OWN], own[...]) + matmul(table[:, OWN:width], landed[...])).astype(BF)


def forward_y_kernel(even, own, xo, xe, table, to_even, to_odd, landed, sent):
    place(even[0], xe, xo, X_ROWS, landed)
    forward(table.at[Y_TABLE:Z_TABLE], own, landed, sent)
    pick(even[1], sent, Y_ROWS, to_even, to_odd)


def forward_z_kernel(even, own, x_landed, yo, ye, table, token, to_even, to_odd, landed, sent):
    landed[0 : 2 * X_ROWS] = x_landed[...]
    place(even[1], ye, yo, Y_ROWS, landed.at[2 * X_ROWS :])
    forward(table.at[Z_TABLE:LEVEL_TABLE], own, landed, sent)
    pick(even[2], sent, Z_ROWS, to_even, to_odd)


def parity_shift(parity, distance):
    total = parity + distance
    return (total & 1, total >> 1) if abs(total >> 1) <= 1 else None


def operator_tiles(ops, dx, dy):
    base = LOOKUP[(dx, dy, -3)] * RANK
    if max(abs(dx), abs(dy)) >= 2:
        return [
            jnp.concatenate(
                [ops[first + RANK : first + 3 * RANK, :], ops[first : first + 2 * RANK, :]], axis=1
            )
            for first in (base, base + 2 * RANK, base + 4 * RANK)
        ]
    zero = jnp.zeros((RANK, RANK), BF)
    op = {dz: ops[base + i * RANK : base + (i + 1) * RANK, :] for i, dz in enumerate((-3, -2, 2, 3))}
    below = jnp.concatenate(
        [jnp.concatenate([op[-2], op[-3]], axis=1), jnp.concatenate([zero, op[-2]], axis=1)], axis=0
    )
    above = jnp.concatenate(
        [jnp.concatenate([op[2], zero], axis=1), jnp.concatenate([op[3], op[2]], axis=1)], axis=0
    )
    return [below, None, above]


def accumulate(source, ops, planes, pairs, targets, distances):
    total = None
    for dx, dy in distances:
        tiles = operator_tiles(ops, dx, dy)
        for pair in pairs:
            if tiles[pair] is None:
                continue
            parts = []
            for plane in planes:
                for target in targets:
                    (qx, cx), (qy, cy) = parity_shift(target[0], dx), parity_shift(target[1], dy)
                    lane = (qx * 2 + qy) * 2 * RANK
                    block = source(cx, cy, plane + pair, slice(lane, lane + 2 * RANK))
                    parts.append(block.reshape(32, 2 * RANK))
            left = jnp.concatenate(parts, axis=0) if len(parts) > 1 else parts[0]
            term = matmul(left, tiles[pair])
            total = term if total is None else total + term
    return total


def interact(source, ops, before, after, planes, pairs, shared, special):
    def add(targets, distances, start):
        total = accumulate(source, ops, planes, pairs, targets, distances)
        for i, plane in enumerate(planes):
            for j, target in enumerate(targets):
                number = TARGETS.index(target)
                first = (i * len(targets) + j) * 32
                part = total[first : first + 32]
                after[plane, number] = part if start is None else start[plane, number] + part

    near, far = range(-2, 3), (3, -3)
    add(TARGETS, [(dx, dy) for dx in near for dy in shared], before)
    for x0 in (0, 1):
        add([(x0, 0), (x0, 1)], [(far[x0], dy) for dy in shared], after)
    for y0 in (0, 1):
        add([(0, y0), (1, y0)], [(dx, dy) for dx in near for dy in special[y0]], after)
    for x0, y0 in TARGETS:
        add([(x0, y0)], [(far[x0], dy) for dy in special[y0]], after)


ALL_PLANES, ALL_PAIRS = range(4), range(3)


def fill(window, table, own, landed):
    width = OWN + landed.shape[0]
    rows = table.shape[0] // 4
    for px in range(4):
        block = table[px * rows : px * rows + rows, :width]
        filled = matmul(block[:, :OWN], own[...]) + matmul(block[:, OWN:], landed[...])
        inside = filled.astype(BF).reshape(window.shape[1], 4, 16, 8 * RANK)
        window[px, :, 1:5] = inside
        window[px, :, 0:1] = jnp.zeros_like(inside[:, :1])
        window[px, :, 5:6] = jnp.zeros_like(inside[:, :1])


def level_kernel(own, landed, table, ops, acc, token, window):
    token[...] = jnp.zeros_like(token)
    fill(window, table.at[LEVEL_TABLE:SIDE_TABLE], own, landed)

    def source(cx, cy, plane, lanes):
        return window[1 + cx : 3 + cx, 0, plane, :, lanes]

    interact(source, ops, None, acc, ALL_PLANES, ALL_PAIRS, [0], ([1], [-1]))


def side_kernel(own, landed, table, expand, ops, level, acc, expand_out, window):
    expand_out[...] = expand[...]
    fill(window, table.at[SIDE_TABLE:OUTER_TABLE], own, landed)

    def source(cx, cy, plane, lanes):
        return window[1 + cx : 3 + cx, (cy + 1) // 2, plane, :, lanes]

    interact(source, ops, level, acc, ALL_PLANES, ALL_PAIRS, [-2, 2], ([-1, 3], [-3, 1]))


def outer_kernel(even, zo, ze, table, expand, ops, inner, out, landed, window, acc, rows):
    place(even[2], ze, zo, Z_ROWS, landed)
    for px in range(4):
        block = table[OUTER_TABLE + px * 96 : OUTER_TABLE + px * 96 + 96, Z_BASE:]
        window[px] = matmul(block, landed[...]).astype(BF).reshape(window.shape[1:])

    def source(cx, cy, plane, lanes):
        return window[1 + cx : 3 + cx, 1 + cy, plane // 5, :, lanes]

    for planes, pairs in (((0,), (0,)), ((3,), (2,))):
        interact(source, ops, inner, acc, planes, pairs, range(-2, 3), ([3], [-3]))
    order = table[ORDER_TABLE : ORDER_TABLE + 128, :128]
    for number, (x0, y0) in enumerate(TARGETS):
        whole = jnp.concatenate(
            [(acc if plane in (0, 3) else inner)[plane, number].astype(BF) for plane in range(4)], axis=0
        )
        ordered = matmul(order, whole)
        for z0 in (0, 1):
            rows[pl.ds(x0 + 2 * y0 + 4 * z0, 128, stride=8), :] = ordered[:, z0 * RANK : z0 * RANK + RANK]
    out[...] = lax.dot_general(
        expand[...], rows[...].astype(BF), (((1,), (1,)), ((), ())), preferred_element_type=F32
    )


VMEM = pl.BlockSpec(memory_space=pltpu.VMEM)
ANY = pl.BlockSpec(memory_space=pl.ANY)
SMEM = pl.BlockSpec(memory_space=pltpu.SMEM)


def rows_of(count):
    return jax.ShapeDtypeStruct((count, 8 * RANK), BF)


def in_hbm(array):
    return pltpu.with_memory_space_constraint(array, pltpu.HBM)


def scratch(*shape, kind=BF):
    return pltpu.VMEM(shape, kind)


def call(kernel, out_shape, scratch_shapes, in_specs, limit=16 << 20, flops=1 << 24, bytes_moved=1 << 20):
    return pl.pallas_call(
        kernel,
        out_shape=out_shape,
        in_specs=in_specs,
        out_specs=jax.tree.map(lambda _: VMEM, out_shape),
        scratch_shapes=scratch_shapes,
        compiler_params=pltpu.CompilerParams(vmem_limit_bytes=limit),
        cost_estimate=pl.CostEstimate(flops=flops, bytes_accessed=bytes_moved, transcendentals=0),
    )


def swap(blocks, bit_list, device_count):
    def position(device):
        return sum((device >> bit & 1) << rank for rank, bit in enumerate(bit_list))

    def move(device, new):
        for rank, bit in enumerate(bit_list):
            device = device & ~(1 << bit) | (new >> rank & 1) << bit
        return device

    extent = 1 << len(bit_list)
    result = []
    for parity, block in enumerate(blocks):
        route = []
        for device in range(device_count):
            at = position(device)
            partner = at + 1 if at % 2 == parity else at - 1
            if 0 <= partner < extent:
                route.append((device, move(device, partner)))
        result.append(lax.ppermute(block, "cells", route))
    return result


def local(multipoles, compress, operators, expand):
    local_bits = multipoles.shape[1].bit_length() - 1
    device_count = lax.axis_size("cells")
    bit_lists = [
        [bit for bit in range(device_count.bit_length() - 1) if (local_bits + bit) % 3 == dimension]
        for dimension in range(3)
    ]
    device = lax.axis_index("cells")
    even = jnp.stack([1 - (device >> bits[0] & 1) for bits in bit_lists]).astype(jnp.int32)

    pair = lambda count: [rows_of(count)] * 2
    tables = [
        send_table(1, Y_ROWS, TABLE),
        send_table(2, Z_ROWS, TABLE),
        window_table((1,), range(1, 5)),
        window_table((0, 2), range(1, 5)),
        window_table(range(3), (0, 5)),
        order_table(),
    ]
    table = jnp.asarray(np.concatenate(tables), BF)
    flat = operators.reshape(-1, RANK)
    own, *send = call(
        compress_kernel,
        [pltpu.VMEM((OWN, 8 * RANK), BF)] + pair(X_ROWS),
        [
            scratch(*multipoles.shape),
            scratch(*compress.shape),
            scratch(1024, RANK, kind=F32),
            scratch(2 * X_ROWS, 8 * RANK),
            pltpu.SemaphoreType.DMA((2,)),
        ],
        [SMEM] + [ANY] * 2,
        flops=FIRST_FLOPS,
    )(even, in_hbm(multipoles), in_hbm(compress))
    x_pair = swap(send, bit_lists[0], device_count)
    ops = flat
    *send, landed = call(
        forward_y_kernel,
        pair(Y_ROWS) + [pltpu.VMEM((2 * X_ROWS, 8 * RANK), BF)],
        [scratch(2 * Y_ROWS, 8 * RANK)],
        [SMEM] + [VMEM] * 4,
    )(even, own, *x_pair[::-1], table)
    y_pair = swap(send, bit_lists[1], device_count)
    sums = (4, 4, 32, 2 * RANK)
    level, token = call(
        level_kernel,
        [pltpu.VMEM(sums, F32), pltpu.VMEM((8, RANK), F32)],
        [scratch(4, 1, 6, 16, 8 * RANK)],
        [VMEM] * 4,
        flops=2 << 30,
    )(own, landed, table, ops)
    *send, landed = call(
        forward_z_kernel,
        pair(Z_ROWS) + [pltpu.VMEM((Z_BASE - OWN, 8 * RANK), BF)],
        [scratch(2 * Z_ROWS, 8 * RANK)],
        [SMEM] + [VMEM] * 6,
    )(even, own, landed, *y_pair[::-1], table, token)
    z_pair = swap(send, bit_lists[2], device_count)
    inner, expand_t = call(
        side_kernel,
        [pltpu.VMEM(sums, F32), pltpu.VMEM(expand.shape[::-1], BF)],
        [scratch(4, 2, 6, 16, 8 * RANK)],
        [VMEM] * 6,
        flops=5 << 30,
    )(own, landed, table, expand.T, ops, level)
    return call(
        outer_kernel,
        jax.ShapeDtypeStruct((expand.shape[1], multipoles.shape[1]), F32),
        [
            scratch(2 * Z_ROWS, 8 * RANK),
            scratch(4, 3, 2, 16, 8 * RANK),
            scratch(*sums, kind=F32),
            scratch(1024, RANK, kind=F32),
        ],
        [SMEM] + [VMEM] * 6,
        flops=2 << 30,
    )(even, *z_pair[::-1], table, expand_t, ops, inner)


def solution(mesh):
    placed = (P(None, "cells"), P(), P(), P())
    return jax.shard_map(
        local, mesh=mesh, in_specs=placed, out_specs=P(None, "cells"), check_vma=False
    )
```
